32 devices in a mesh: tr: 16 (over z, y, x), ct: 2 (over core).
Axes of the slice: x: 2, y: 2, z: 4, core: 2. Of those that a mesh axis runs over, the one named last changes fastest.
Arguments:
- amplitudes: bfloat16 [8, 1024, 2, 1024], P(None, 'tr', None, 'ct'), may hold values from -6 to 6
- cycle_integrals: bfloat16 [2, 1024, 1, 1024], P(None, 'ct', None, 'tr'), may hold values from -0.125 to 0.125
- pair_live: int32 [8, 16], replicated, may hold values 0 or 1
Outputs:
- permuted: bfloat16 [8, 1024, 1, 1024], P('ct', 'tr')
The draws below stay inside these ranges and needn't reach their ends.
All inputs are finite; a program needn't handle non-finite values.
Results may differ from the reference program's by a relative error of at most 0.017.
Values may be sent and summed in bfloat16 or wider, within the bound.
No kernel may reach another device: no remote copies, remote signals or barrier semaphores. Data moves between devices by JAX's collectives and lax.ppermute only.
A program may use at most 64 MiB of HBM per device.

```python
import jax
import jax.numpy as jnp
from jax import lax

VT = 64
NI = 8
NK = 2
NJ = 1
NV = 16
V = 1024
N_CT = 2


def set_ends(result, own_key, smallest, top_value):
    spot = [jax.random.randint(jax.random.fold_in(own_key, axis), (), 0, length) for axis, length in enumerate(result.shape)]
    longest = result.shape.index(max(result.shape))
    neighbour = spot[:longest] + [(spot[longest] + 1) % result.shape[longest]] + spot[longest + 1:]
    return result.at[tuple(spot)].set(smallest).at[tuple(neighbour)].set(top_value)


def with_spikes(result, own_key, source, target, parts, factor):
    owner, partner = [(jnp.arange(result.shape[axis_at]) // (result.shape[axis_at] // parts)).reshape([-1 if axis == axis_at else 1 for axis in range(result.ndim)]) for axis_at in (source, target)]
    chosen = jax.random.permutation(own_key, parts)[partner]
    strong = (owner == chosen) | (owner == (partner + parts // 2) % parts)
    return jnp.where(strong, factor * result, result)


def level_of(key, extent, pieces, smallest, high):
    loudness, own = 1.0, jax.random.fold_in(key, 6)
    for dim, blocks in pieces:
        heights = jnp.exp(jax.random.uniform(jax.random.fold_in(own, dim), (blocks,), jnp.float32, smallest / len(pieces), high / len(pieces)))
        loudness = loudness * jnp.repeat(heights, extent[dim] // blocks).reshape([-1 if axis == dim else 1 for axis in range(len(extent))])
    return loudness


def bell_draw(rng, shape, width, bound, cuts=(), kind=jnp.bfloat16):
    gain = level_of(rng, shape, cuts, -0.22, 0.18) if cuts else 1.0
    result = jax.random.normal(rng, shape, jnp.float32) * width * gain
    return jnp.minimum(jnp.maximum(result, -bound), bound).astype(kind)


def heavy_noise(own_key, dims, deviation, bound, cuts, heavy, dtype=jnp.bfloat16):
    result = deviation * jax.random.normal(own_key, dims, jnp.float32)
    if cuts:
        result = result * level_of(own_key, dims, cuts, -0.22, 0.18)
    return jnp.clip(with_spikes(result, jax.random.fold_in(own_key, 3), *heavy), -bound, bound).astype(dtype)


def setup_inputs(seed: int = 0) -> dict:
    keys = jax.random.split(jax.random.key(seed), 4)
    amplitudes = heavy_noise(keys[0], (NI, V, NK, V), 1.0, 6.0, ((1, 16), (3, 2)), (3, 0, 2, 2.0))
    cycle_integrals = bell_draw(keys[1], (NK, V, NJ, V), (NK * V) ** -0.5, 0.125, ((1, 2), (3, 16)))
    pair_live = set_ends((jax.random.randint(keys[2], (NI, NV), 0, 4) < 3).astype(jnp.int32), jax.random.fold_in(keys[2], 1), 0, 1)
    return {"amplitudes": amplitudes, "cycle_integrals": cycle_integrals, "pair_live": pair_live}


def reference(amplitudes, cycle_integrals, pair_live):
    row_live = jnp.repeat(pair_live, VT, axis=1).astype(jnp.bfloat16)
    col_live = row_live[:NK]
    masked = amplitudes * row_live[:, :, None, None] * col_live[None, None, :, :]
    per_block = V // N_CT

    def block_term(group, totals):
        offset = (group * per_block).astype(jnp.int32)
        amp_blk = lax.dynamic_slice_in_dim(masked, offset, per_block, 3).astype(jnp.float32)
        int_blk = lax.dynamic_slice_in_dim(cycle_integrals, offset, per_block, 1).astype(jnp.float32)
        product = jnp.einsum('iakc,kcjb->iajb', amp_blk, int_blk)
        rounded = lax.optimization_barrier(product.astype(jnp.bfloat16))
        return totals + rounded.astype(jnp.float32)

    start_sum = jnp.zeros((NI, V, NJ, V), jnp.float32)
    totals = lax.fori_loop(jnp.int32(0), jnp.int32(N_CT), block_term, start_sum)
    cycle = totals.astype(jnp.bfloat16)
    return jnp.transpose(cycle, (0, 3, 2, 1))
```

```python
import functools

import jax
import jax.numpy as jnp
from jax import lax
from jax.experimental import pallas as pl
from jax.experimental.pallas import tpu as pltpu
from jax.sharding import PartitionSpec as P

F32 = jnp.float32
VMEM = pl.BlockSpec(memory_space=pltpu.VMEM)
SMEM = pl.BlockSpec(memory_space=pltpu.SMEM)
PARAMS = pltpu.CompilerParams(vmem_limit_bytes=48 * 1024 * 1024)


def partials_kernel(n_ct, place, live, *refs):
    mine, theirs, tiles, outs = refs[0], refs[1], refs[2:-n_ct], refs[-n_ct:]
    tr, ct = place[0], place[1]
    n_i, n_k, vt, cols = mine.shape
    n_local = n_i // n_ct
    first = (tr % 2) == 0
    even = (tr // 2) * 2
    col_tile = lax.broadcasted_iota(jnp.int32, (1, cols), 1) // vt
    col_masks = []
    for k in range(n_k):
        mask = jnp.zeros((1, cols), F32)
        for t in range(cols // vt):
            kept = live[k, ct * (cols // vt) + t].astype(F32)
            mask = jnp.where(col_tile == t, kept, mask)
        col_masks.append(mask.astype(jnp.bfloat16))
    lhs = []
    for k in range(n_k):
        stacked = jnp.concatenate([ref[s, k] for ref in tiles for s in range(ref.shape[0])], axis=0)
        lhs.append(stacked * col_masks[k])
    half = lax.broadcasted_iota(jnp.int32, (1, 2 * vt), 1) < vt
    entries = [(e, local) for e in range(n_ct) for local in range(n_local)]
    for at in range(0, n_i, 2):
        total = None
        for k in range(n_k):
            rows = []
            for e, local in entries[at : at + 2]:
                i = (ct ^ e) * n_local + local
                own, other = mine[i, k], theirs[i, k]
                rows += [jnp.where(first, own, other), jnp.where(first, other, own)]
            term = lax.dot_general(
                lhs[k],
                jnp.concatenate(rows, axis=0),
                (((1,), (1,)), ((), ())),
                preferred_element_type=F32,
            )
            total = term if total is None else total + term
        for n, (e, local) in enumerate(entries[at : at + 2]):
            i = (ct ^ e) * n_local + local
            row_mask = jnp.where(half, live[i, even].astype(F32), live[i, even + 1].astype(F32))
            outs[e][local] = (total[:, n * 2 * vt : (n + 1) * 2 * vt] * row_mask).astype(outs[e].dtype)


def add_kernel(n_parts, *refs):
    parts, outs = refs[:n_parts], refs[n_parts:]
    vt = outs[0].shape[1]
    for d, out in enumerate(outs):
        total = parts[0][:, pl.ds(d * vt, vt)].astype(F32)
        for part in parts[1:]:
            total += part[:, pl.ds(d * vt, vt)].astype(F32)
        out[...] = total.astype(out.dtype)


def place_kernel(offsets, place, *refs):
    parts, out = refs[:-1], refs[-1]
    width = parts[0].shape[2]
    pair = place[0] // 2
    for d, part in zip(offsets, parts, strict=True):
        at = pl.multiple_of((pair ^ (d // 2)) * width, width)
        out[:, :, pl.ds(at, width)] = part[...]


def per_device(n_tr, n_ct, amplitudes, cycle_integrals, pair_live):
    n_i, vt, n_k, cols = amplitudes.shape
    n_j = cycle_integrals.shape[2]
    n_local = n_i // n_ct
    tr, ct = lax.axis_index("tr"), lax.axis_index("ct")
    place = jnp.stack([tr, ct]).astype(jnp.int32)

    def swap(value, d, axis="tr", size=n_tr):
        return lax.ppermute(value, axis, [(n, n ^ d) for n in range(size)])

    own_w = jnp.transpose(cycle_integrals, (2, 0, 3, 1))
    other = swap(amplitudes, 1)
    far = list(range(4, n_tr, 4))
    arrived = [swap(own_w, d) for d in far]
    near = swap(own_w, 2)
    forwarded = [swap(w, 2) for w in arrived]
    tiles = [own_w, near] + [w for both in zip(arrived, forwarded) for w in both]
    offsets = [0, 2] + [d + y for d in far for y in (0, 2)]

    rows = len(tiles) * vt
    partials = pl.pallas_call(
        functools.partial(partials_kernel, n_ct),
        out_shape=[jax.ShapeDtypeStruct((n_local, rows, 2 * vt), jnp.bfloat16)] * n_ct,
        in_specs=[SMEM, SMEM] + [VMEM] * (2 + len(tiles)),
        out_specs=[VMEM] * n_ct,
        compiler_params=PARAMS,
    )(place, pair_live, jnp.transpose(amplitudes, (0, 2, 1, 3)), jnp.transpose(other, (0, 2, 1, 3)), *tiles)

    parts = [partials[0]] + [swap(partials[e], e, "ct", n_ct) for e in range(1, n_ct)]
    blocks = pl.pallas_call(
        functools.partial(add_kernel, n_ct),
        out_shape=[jax.ShapeDtypeStruct((n_local, vt, 2 * vt), jnp.bfloat16)] * len(tiles),
        in_specs=[VMEM] * n_ct,
        out_specs=[VMEM] * len(tiles),
        compiler_params=PARAMS,
    )(*parts)
    moved = [b if d == 0 else swap(b, d) for d, b in zip(offsets, blocks)]
    result = pl.pallas_call(
        functools.partial(place_kernel, offsets),
        out_shape=jax.ShapeDtypeStruct((n_local, vt, n_tr * vt), jnp.bfloat16),
        in_specs=[SMEM] + [VMEM] * len(moved),
        out_specs=VMEM,
        compiler_params=PARAMS,
    )(place, *moved)
    return result.reshape(n_local, vt, n_j, n_tr * vt)


def solution(mesh):
    return jax.shard_map(
        functools.partial(per_device, mesh.shape["tr"], mesh.shape["ct"]),
        mesh=mesh,
        in_specs=(P(None, "tr", None, "ct"), P(None, "ct", None, "tr"), P()),
        out_specs=P("ct", "tr", None, None),
        check_vma=False,
    )
```

```python
import functools

import jax
import jax.numpy as jnp
from jax import lax
from jax.experimental import pallas as pl
from jax.experimental.pallas import tpu as pltpu
from jax.sharding import PartitionSpec as P

F32 = jnp.float32
VMEM = pl.BlockSpec(memory_space=pltpu.VMEM)
ANY = pl.BlockSpec(memory_space=pl.ANY)
SMEM = pl.BlockSpec(memory_space=pltpu.SMEM)
BIG = pl.CostEstimate(flops=10_000_000_000, bytes_accessed=1, transcendentals=0)
WAIT = pl.CostEstimate(flops=3_000_000_000, bytes_accessed=1, transcendentals=0)
COST = pl.CostEstimate(flops=1, bytes_accessed=1, transcendentals=0)
PARAMS = pltpu.CompilerParams(vmem_limit_bytes=16 * 1024 * 1024)


def pair_bit(ct):
    return 1 + ct % 2


def masks_kernel(n_ct, n_k, n_local, vt, live, out):
    tr, ct = lax.axis_index("tr"), lax.axis_index("ct")
    cols = out.shape[1]
    bit = pair_bit(ct)
    turned = (bit == 2) & ((tr & 1) == 1)
    members = [(tr & ~bit) + jnp.where(turned, bit, 0), (tr & ~bit) + jnp.where(turned, 0, bit)]
    tile = lax.broadcasted_iota(jnp.int32, (1, cols), 1) // vt
    for e in range(n_ct):
        for k in range(n_k):
            mask = jnp.zeros((1, cols), F32)
            for t in range(cols // vt):
                mask = jnp.where(tile == t, live[k, (ct ^ e) * (cols // vt) + t].astype(F32), mask)
            out[pl.ds(e * n_k + k, 1)] = mask
    for i in range(n_local):
        row = ct * n_local + i
        both = jnp.where(tile < 1, live[row, members[0]].astype(F32), live[row, members[1]].astype(F32))
        out[pl.ds(n_ct * n_k + i, 1)] = both
    out[pl.ds(n_ct * n_k + n_local, 1)] = jnp.full((1, cols), (members[0] == tr).astype(F32))


def blocks_kernel(n_ct, own_at, their_at, tiles_at, masks, *refs):
    outs = refs[-len(tiles_at) :]
    n_local, n_k, vt, cols = refs[own_at[0][0]].shape[1:]
    first = masks[pl.ds(n_ct * n_k + n_local, 1)] > 0
    lhs = {}
    for e in range(n_ct):
        for k in range(n_k):
            stacked = jnp.concatenate([refs[n][at, k] for n, at in (tile[e] for tile in tiles_at)], axis=0)
            lhs[e, k] = stacked * masks[pl.ds(e * n_k + k, 1)].astype(jnp.bfloat16)
    step = min(2, n_local)
    for start in range(0, n_local, step):
        total = None
        for (e, k), left in lhs.items():
            rows = []
            for i in range(start, start + step):
                a, b = (refs[n][at, i, k] for n, at in (own_at[e], their_at[e]))
                rows += [jnp.where(first, a, b), jnp.where(first, b, a)]
            term = lax.dot_general(
                left,
                jnp.concatenate(rows, axis=0),
                (((1,), (1,)), ((), ())),
                preferred_element_type=F32,
            )
            total = term if total is None else total + term
        for i in range(start, start + step):
            row_mask = masks[pl.ds(n_ct * n_k + i, 1), pl.ds(0, 2 * vt)]
            kept = total[:, (i - start) * 2 * vt : (i - start + 1) * 2 * vt] * row_mask
            for d, out in enumerate(outs):
                out[i] = kept[d * vt : (d + 1) * vt].astype(out.dtype)


def place_kernel(shifts, order, *refs):
    parts, (out, stage, sems) = dict(zip(order, refs)), refs[-3:]
    tr, ct = lax.axis_index("tr"), lax.axis_index("ct")
    wide = parts[0].shape[2]
    half = lax.broadcasted_iota(jnp.int32, (1, wide), 1) < wide // 2
    straight = pair_bit(ct) == 1
    own_first = (tr & (3 - pair_bit(ct))) == 0
    copies = []
    for n, by_core in enumerate(shifts):
        shift = sum(jnp.where(ct == c, z, 0) for c, z in enumerate(by_core))
        at = pl.multiple_of(((tr // 4) ^ shift) * 2 * wide, 2 * wide)
        for i in range(out.shape[0]):
            a, b = parts[2 * n][i], parts[2 * n + 1][i]
            lo, hi = jnp.where(own_first, a, b), jnp.where(own_first, b, a)
            across = pltpu.roll(jnp.where(half, hi, lo).astype(F32), wide // 2, 1).astype(lo.dtype)
            stage[n, i, :, pl.ds(0, wide)] = jnp.where(straight, lo, jnp.where(half, lo, hi))
            stage[n, i, :, pl.ds(wide, wide)] = jnp.where(straight, hi, across)
        copies.append(pltpu.make_async_copy(stage.at[n], out.at[:, :, pl.ds(at, 2 * wide)], sems.at[n]))
        copies[-1].start()
    for copy in copies:
        copy.wait()


def per_device(n_tr, n_ct, amplitudes, cycle_integrals, pair_live):
    n_i, vt, n_k, cols = amplitudes.shape
    n_j = cycle_integrals.shape[2]
    n_local = n_i // n_ct
    tr, ct = lax.axis_index("tr"), lax.axis_index("ct")

    def over_ct(value, e):
        return lax.ppermute(value, "ct", [(c, c ^ e) for c in range(n_ct)])

    def over_tr(value, move, e=0):
        pairs = [(r * n_ct + c, (r ^ move(c ^ e)) * n_ct + (c ^ e)) for r in range(n_tr) for c in range(n_ct)]
        return lax.ppermute(value, ("tr", "ct"), pairs)

    def gathered(value):
        return [value] + [over_ct(value, e) for e in range(1, n_ct)]

    own_w = jnp.transpose(cycle_integrals, (2, 0, 3, 1))
    n_z = n_tr // 4
    far = sorted(range(1, n_z), key=lambda z: -z)
    shared, split = far[: len(far) // n_ct * n_ct], far[len(far) // n_ct * n_ct :]
    groups = [shared[n : n + n_ct] for n in range(0, len(shared), n_ct)]
    shifts = [[group[c ^ e] for c in range(n_ct)] for group in groups for e in range(n_ct)]
    shifts += [[z] * n_ct for z in split] + [[0] * n_ct]

    def beside(c):
        return 3 - pair_bit(c)

    def pack(parts, after=(), cost=COST):
        def kernel(*refs):
            out, at = refs[-1], 0
            for ref in refs[: len(parts)]:
                out[pl.ds(at, ref.shape[0])] = ref[...]
                at += ref.shape[0]

        return pl.pallas_call(
            kernel,
            out_shape=jax.ShapeDtypeStruct((sum(p.shape[0] for p in parts), *parts[0].shape[1:]), parts[0].dtype),
            in_specs=[VMEM] * len(parts) + [ANY] * len(after),
            out_specs=VMEM,
            compiler_params=PARAMS,
            cost_estimate=cost,
        )(*parts, *after)

    masks = pl.pallas_call(
        functools.partial(masks_kernel, n_ct, n_k, n_local, vt),
        out_shape=jax.ShapeDtypeStruct((n_ct * n_k + n_local + 1, cols), F32),
        in_specs=[SMEM],
        out_specs=VMEM,
        compiler_params=PARAMS,
        cost_estimate=COST,
    )(pair_live)
    by_group = jnp.transpose(amplitudes, (0, 2, 1, 3)).reshape(n_ct, n_local, n_k, vt, cols)
    given = [lax.dynamic_index_in_dim(by_group, ct ^ e, 0) for e in range(n_ct)]
    own_a = [given[0]] + [over_ct(given[e], e) for e in range(1, n_ct)]
    own_parts = pack(gathered(own_w))
    whole = [over_tr(own_parts, lambda c, group=group: 4 * group[c]) for group in groups]
    some = [over_tr(own_w, lambda c, z=z: 4 * z) for z in split]
    their_a = [over_tr(value, pair_bit, e) for e, value in enumerate(given)]
    whole = pack(whole, [masks], WAIT)
    whole_rest = [over_ct(whole, e) for e in range(1, n_ct)]
    whole_side = [over_tr(whole, beside, e) for e in range(n_ct)]
    some = pack([own_w, *some], [])
    some_rest = [over_ct(some, e) for e in range(1, n_ct)]
    some_side = [over_tr(some, beside, e) for e in range(n_ct)]

    group_tiles = [[(n, g * n_ct + (e ^ n)) for e in range(n_ct)] for g in range(len(groups)) for n in range(n_ct)]
    split_tiles = [[(n_ct + e, n) for e in range(n_ct)] for n in [*range(1, len(split) + 1), 0]]

    def blocks(tiles, arrays, after=(), cost=COST):
        used = sorted({n for tile in tiles for n, _ in tile})
        arrays = [*own_a, *their_a, *[arrays[n] for n in used]]
        own_at, their_at = [(e, 0) for e in range(n_ct)], [(n_ct + e, 0) for e in range(n_ct)]
        tiles_at = [[(2 * n_ct + used.index(n), at) for n, at in tile] for tile in tiles]
        return pl.pallas_call(
            functools.partial(blocks_kernel, n_ct, own_at, their_at, tiles_at),
            out_shape=[jax.ShapeDtypeStruct((n_local, vt, 2 * vt), jnp.bfloat16)] * len(tiles),
            in_specs=[VMEM] * (1 + len(arrays)) + [ANY] * len(after),
            out_specs=[VMEM] * len(tiles),
            compiler_params=PARAMS,
            cost_estimate=cost,
        )(masks, *arrays, *after)

    near = blocks(group_tiles + split_tiles, [whole, *whole_rest, some, *some_rest])
    near_made = near
    near = [over_tr(b, lambda c, by=by: 4 * by[c]) if any(by) else b for b, by in zip(near, shifts)]
    side = blocks(group_tiles, whole_side, near[:1], WAIT)
    side += blocks(split_tiles, [None] * n_ct + some_side, [side[0], *near[:-1]], WAIT)
    side = [over_tr(b, lambda c, by=by: 4 * by[c] + beside(c)) for b, by in zip(side, shifts)]
    moved = [b for both in zip(near, side) for b in both]
    order = list(range(len(moved)))
    result = pl.pallas_call(
        functools.partial(place_kernel, shifts, order),
        out_shape=jax.ShapeDtypeStruct((n_local, vt, n_tr * vt), jnp.bfloat16),
        in_specs=[VMEM] * len(moved),
        out_specs=ANY,
        scratch_shapes=[
            pltpu.VMEM((n_z, n_local, vt, 4 * vt), jnp.bfloat16),
            pltpu.SemaphoreType.DMA((n_z,)),
        ],
        compiler_params=PARAMS,
        cost_estimate=COST,
    )(*[moved[n] for n in order])
    return result.reshape(n_local, vt, n_j, n_tr * vt)


def solution(mesh):
    return jax.shard_map(
        functools.partial(per_device, mesh.shape["tr"], mesh.shape["ct"]),
        mesh=mesh,
        in_specs=(P(None, "tr", None, "ct"), P(None, "ct", None, "tr"), P()),
        out_specs=P("ct", "tr", None, None),
        check_vma=False,
    )
```

```python
import functools

import jax
import jax.numpy as jnp
from jax import lax
from jax.experimental import pallas as pl
from jax.experimental.pallas import tpu as pltpu
from jax.sharding import PartitionSpec as P

F32 = jnp.float32
VMEM = pl.BlockSpec(memory_space=pltpu.VMEM)
ANY = pl.BlockSpec(memory_space=pl.ANY)
SMEM = pl.BlockSpec(memory_space=pltpu.SMEM)
PARAMS = pltpu.CompilerParams(vmem_limit_bytes=16 * 1024 * 1024)


def cost(gflop=0):
    return pl.CostEstimate(flops=1 + gflop * 1_000_000_000, bytes_accessed=1, transcendentals=0)


def pair_bit(ct):
    return 1 + ct % 2


def masks_kernel(n_ct, n_k, n_local, vt, live, out):
    tr, ct = lax.axis_index("tr"), lax.axis_index("ct")
    cols = out.shape[1]
    bit = pair_bit(ct)
    turned = (bit == 2) & ((tr & 1) == 1)
    members = [(tr & ~bit) + jnp.where(turned, bit, 0), (tr & ~bit) + jnp.where(turned, 0, bit)]
    tile = lax.broadcasted_iota(jnp.int32, (1, cols), 1) // vt
    for e in range(n_ct):
        for k in range(n_k):
            mask = jnp.zeros((1, cols), F32)
            for t in range(cols // vt):
                mask = jnp.where(tile == t, live[k, (ct ^ e) * (cols // vt) + t].astype(F32), mask)
            out[pl.ds(e * n_k + k, 1)] = mask
    for i in range(n_local):
        row = ct * n_local + i
        both = jnp.where(tile < 1, live[row, members[0]].astype(F32), live[row, members[1]].astype(F32))
        out[pl.ds(n_ct * n_k + i, 1)] = both
    out[pl.ds(n_ct * n_k + n_local, 1)] = jnp.full((1, cols), (members[0] == tr).astype(F32))


def pack_kernel(count, *refs):
    out, at = refs[-1], 0
    for ref in refs[:count]:
        out[pl.ds(at, ref.shape[0])] = ref[...]
        at += ref.shape[0]


def blocks_kernel(n_ct, tiles_at, masks, *refs):
    own, theirs, arrays, outs = refs[:n_ct], refs[n_ct : 2 * n_ct], refs[2 * n_ct :], refs[-len(tiles_at) :]
    n_local, n_k, vt, cols = own[0].shape[1:]
    first = masks[pl.ds(n_ct * n_k + n_local, 1)] > 0
    lhs = {}
    for e in range(n_ct):
        for k in range(n_k):
            stacked = jnp.concatenate([arrays[n][at, k] for n, at in (tile[e] for tile in tiles_at)], axis=0)
            lhs[e, k] = stacked * masks[pl.ds(e * n_k + k, 1)].astype(jnp.bfloat16)
    step = min(2, n_local)
    for start in range(0, n_local, step):
        total = None
        for (e, k), left in lhs.items():
            rows = []
            for i in range(start, start + step):
                a, b = own[e][0, i, k], theirs[e][0, i, k]
                rows += [jnp.where(first, a, b), jnp.where(first, b, a)]
            term = lax.dot_general(
                left,
                jnp.concatenate(rows, axis=0),
                (((1,), (1,)), ((), ())),
                preferred_element_type=F32,
            )
            total = term if total is None else total + term
        for i in range(start, start + step):
            row_mask = masks[pl.ds(n_ct * n_k + i, 1), pl.ds(0, 2 * vt)]
            kept = total[:, (i - start) * 2 * vt : (i - start + 1) * 2 * vt] * row_mask
            for d, out in enumerate(outs):
                out[i] = kept[d * vt : (d + 1) * vt].astype(out.dtype)


def join_kernel(*refs):
    refs[-1][...] = jnp.zeros_like(refs[-1])


def place_kernel(shifts, *refs):
    parts, (out, stage, sems) = refs, refs[-3:]
    tr, ct = lax.axis_index("tr"), lax.axis_index("ct")
    wide = parts[0].shape[2]
    half = lax.broadcasted_iota(jnp.int32, (1, wide), 1) < wide // 2
    straight = pair_bit(ct) == 1
    own_first = (tr & (3 - pair_bit(ct))) == 0
    copies = []
    for n, by_core in enumerate(shifts):
        shift = sum(jnp.where(ct == c, z, 0) for c, z in enumerate(by_core))
        at = pl.multiple_of(((tr // 4) ^ shift) * 2 * wide, 2 * wide)
        for i in range(out.shape[0]):
            a, b = parts[2 * n][i], parts[2 * n + 1][i]
            lo, hi = jnp.where(own_first, a, b), jnp.where(own_first, b, a)
            across = pltpu.roll(jnp.where(half, hi, lo).astype(F32), wide // 2, 1).astype(lo.dtype)
            stage[n, i, :, pl.ds(0, wide)] = jnp.where(straight, lo, jnp.where(half, lo, hi))
            stage[n, i, :, pl.ds(wide, wide)] = jnp.where(straight, hi, across)
        copies.append(pltpu.make_async_copy(stage.at[n], out.at[:, :, pl.ds(at, 2 * wide)], sems.at[n]))
        copies[-1].start()
    for copy in copies:
        copy.wait()


def per_device(n_tr, n_ct, amplitudes, cycle_integrals, pair_live):
    n_i, vt, n_k, cols = amplitudes.shape
    n_j = cycle_integrals.shape[2]
    n_local = n_i // n_ct
    n_z = n_tr // 4
    ct = lax.axis_index("ct")
    far = sorted(range(1, n_z), key=lambda z: -z)
    shared, split = far[: len(far) // n_ct * n_ct], far[len(far) // n_ct * n_ct :]
    groups = [shared[n : n + n_ct] for n in range(0, len(shared), n_ct)]
    shifts = [[group[c ^ e] for c in range(n_ct)] for group in groups for e in range(n_ct)]
    shifts += [[z] * n_ct for z in split] + [[0] * n_ct]

    def beside(c):
        return 3 - pair_bit(c)

    def over_ct(value, e):
        return lax.ppermute(value, "ct", [(c, c ^ e) for c in range(n_ct)])

    def over_tr(value, move, e=0):
        pairs = [(r * n_ct + c, (r ^ move(c ^ e)) * n_ct + (c ^ e)) for r in range(n_tr) for c in range(n_ct)]
        return lax.ppermute(value, ("tr", "ct"), pairs)

    def call(kernel, shape, inputs, after=(), gflop=0, dtype=jnp.bfloat16, count=None):
        result = jax.ShapeDtypeStruct(shape, dtype)
        return pl.pallas_call(
            kernel,
            out_shape=result if count is None else [result] * count,
            in_specs=[VMEM] * len(inputs) + [ANY] * len(after),
            out_specs=VMEM if count is None else [VMEM] * count,
            compiler_params=PARAMS,
            cost_estimate=cost(gflop),
        )(*inputs, *after)

    def pack(parts, after=(), gflop=0):
        shape = (sum(part.shape[0] for part in parts), *parts[0].shape[1:])
        return call(functools.partial(pack_kernel, len(parts)), shape, parts, after, gflop)

    own_w = jnp.transpose(cycle_integrals, (2, 0, 3, 1))
    masks = pl.pallas_call(
        functools.partial(masks_kernel, n_ct, n_k, n_local, vt),
        out_shape=jax.ShapeDtypeStruct((n_ct * n_k + n_local + 1, cols), F32),
        in_specs=[SMEM],
        out_specs=VMEM,
        compiler_params=PARAMS,
        cost_estimate=cost(),
    )(pair_live)

    by_group = jnp.transpose(amplitudes, (0, 2, 1, 3)).reshape(n_ct, n_local, n_k, vt, cols)
    given = [lax.dynamic_index_in_dim(by_group, ct ^ e, 0) for e in range(n_ct)]
    own_a = [given[0]] + [over_ct(given[e], e) for e in range(1, n_ct)]

    own_parts = pack([own_w] + [over_ct(own_w, e) for e in range(1, n_ct)], [given[0]])
    some = [over_tr(own_w, lambda c, z=z: 4 * z) for z in split]
    whole = [over_tr(own_parts, lambda c, group=group: 4 * group[c]) for group in groups]
    their_a = [over_tr(value, pair_bit, e) for e, value in enumerate(given)]
    whole = pack(whole, [masks, *some], 3)
    some = some[0] if len(some) == 1 else pack(some)
    whole_rest = [over_ct(whole, e) for e in range(1, n_ct)]
    whole_side = over_tr(pack([whole, *whole_rest]), beside)
    some_rest = [over_ct(some, e) for e in range(1, n_ct)]
    some_side = over_tr(pack([own_parts, some, *some_rest], their_a), beside)

    n_whole, n_some = whole.shape[0], some.shape[0]
    of_group = [[(n, g * n_ct + (e ^ n)) for e in range(n_ct)] for g in range(len(groups)) for n in range(n_ct)]
    column = of_group + [[(n_ct + e, n) for e in range(n_ct)] for n in range(len(split))]
    column += [[(2 * n_ct, e) for e in range(n_ct)]]
    side_far = [[(0, n * n_whole + at) for n, at in tile] for tile in of_group]
    side_near = [[(0, n_ct + e * n_some + n) for e in range(n_ct)] for n in range(len(split))]
    side_near += [[(0, e) for e in range(n_ct)]]

    def blocks(tiles, arrays, after, gflop):
        kernel = functools.partial(blocks_kernel, n_ct, tiles)
        inputs = [masks, *own_a, *their_a, *arrays]
        return call(kernel, (n_local, vt, 2 * vt), inputs, after, gflop, count=len(tiles))

    near = blocks(column, [whole, *whole_rest, some, *some_rest, own_parts], [], 5)
    made = near[:1]
    near = [over_tr(b, lambda c, by=by: 4 * by[c]) if any(by) else b for b, by in zip(near, shifts)]
    side = blocks(side_far, [whole_side], made, 6)
    made = side[:1]
    side = [over_tr(b, lambda c, by=by: 4 * by[c] + beside(c)) for b, by in zip(side, shifts)]
    late = blocks(side_near, [some_side], [*made, *near[:2]], 3)
    done = call(join_kernel, (8, 128), [], side, 10, F32)
    side += [over_tr(b, lambda c, by=by: 4 * by[c] + beside(c)) for b, by in zip(late, shifts[len(shared) :])]

    moved = [block for both in zip(near, side) for block in both]
    result = pl.pallas_call(
        functools.partial(place_kernel, shifts),
        out_shape=jax.ShapeDtypeStruct((n_local, vt, n_tr * vt), jnp.bfloat16),
        in_specs=[VMEM] * len(moved) + [ANY],
        out_specs=ANY,
        scratch_shapes=[
            pltpu.VMEM((n_z, n_local, vt, 4 * vt), jnp.bfloat16),
            pltpu.SemaphoreType.DMA((n_z,)),
        ],
        compiler_params=PARAMS,
        cost_estimate=cost(),
    )(*moved, done)
    return result.reshape(n_local, vt, n_j, n_tr * vt)


def solution(mesh):
    return jax.shard_map(
        functools.partial(per_device, mesh.shape["tr"], mesh.shape["ct"]),
        mesh=mesh,
        in_specs=(P(None, "tr", None, "ct"), P(None, "ct", None, "tr"), P()),
        out_specs=P("ct", "tr", None, None),
        check_vma=False,
    )
```

```python
import functools

import jax
import jax.numpy as jnp
from jax import lax
from jax.experimental import pallas as pl
from jax.experimental.pallas import tpu as pltpu
from jax.sharding import PartitionSpec as P

F32 = jnp.float32
VMEM = pl.BlockSpec(memory_space=pltpu.VMEM)
ANY = pl.BlockSpec(memory_space=pl.ANY)
SMEM = pl.BlockSpec(memory_space=pltpu.SMEM)
PARAMS = pltpu.CompilerParams(vmem_limit_bytes=16 * 1024 * 1024)


def cost(gflop=0):
    return pl.CostEstimate(flops=1 + gflop * 1_000_000_000, bytes_accessed=1, transcendentals=0)


def pair_bit(ct):
    return 1 + ct % 2


def masks_kernel(n_ct, n_k, n_local, vt, live, out):
    tr, ct = lax.axis_index("tr"), lax.axis_index("ct")
    cols = out.shape[1]
    bit = pair_bit(ct)
    turned = (bit == 2) & ((tr & 1) == 1)
    members = [(tr & ~bit) + jnp.where(turned, bit, 0), (tr & ~bit) + jnp.where(turned, 0, bit)]
    tile = lax.broadcasted_iota(jnp.int32, (1, cols), 1) // vt
    for e in range(n_ct):
        for k in range(n_k):
            mask = jnp.zeros((1, cols), F32)
            for t in range(cols // vt):
                mask = jnp.where(tile == t, live[k, (ct ^ e) * (cols // vt) + t].astype(F32), mask)
            out[pl.ds(e * n_k + k, 1)] = mask
    for i in range(n_local):
        row = ct * n_local + i
        both = jnp.where(tile < 1, live[row, members[0]].astype(F32), live[row, members[1]].astype(F32))
        out[pl.ds(n_ct * n_k + i, 1)] = both
    out[pl.ds(n_ct * n_k + n_local, 1)] = jnp.full((1, cols), (members[0] == tr).astype(F32))


def pack_kernel(count, *refs):
    out, at = refs[-1], 0
    for ref in refs[:count]:
        out[pl.ds(at, ref.shape[0])] = ref[...]
        at += ref.shape[0]


def blocks_kernel(n_ct, tiles_at, masks, *refs):
    own, theirs, arrays, outs = refs[:n_ct], refs[n_ct : 2 * n_ct], refs[2 * n_ct :], refs[-len(tiles_at) :]
    n_local, n_k, vt, cols = own[0].shape[1:]
    first = masks[pl.ds(n_ct * n_k + n_local, 1)] > 0
    lhs = {}
    for e in range(n_ct):
        for k in range(n_k):
            stacked = jnp.concatenate([arrays[n][at, k] for n, at in (tile[e] for tile in tiles_at)], axis=0)
            lhs[e, k] = stacked * masks[pl.ds(e * n_k + k, 1)].astype(jnp.bfloat16)
    step = min(2, n_local)
    for start in range(0, n_local, step):
        total = None
        for (e, k), left in lhs.items():
            rows = []
            for i in range(start, start + step):
                a, b = own[e][0, i, k], theirs[e][0, i, k]
                rows += [jnp.where(first, a, b), jnp.where(first, b, a)]
            term = lax.dot_general(
                left,
                jnp.concatenate(rows, axis=0),
                (((1,), (1,)), ((), ())),
                preferred_element_type=F32,
            )
            total = term if total is None else total + term
        for i in range(start, start + step):
            row_mask = masks[pl.ds(n_ct * n_k + i, 1), pl.ds(0, 2 * vt)]
            kept = total[:, (i - start) * 2 * vt : (i - start + 1) * 2 * vt] * row_mask
            for d, out in enumerate(outs):
                out[i] = kept[d * vt : (d + 1) * vt].astype(out.dtype)


def join_kernel(*refs):
    refs[-1][...] = jnp.zeros_like(refs[-1])


def place_kernel(shifts, *refs):
    parts, (out, stage, sems) = refs, refs[-3:]
    tr, ct = lax.axis_index("tr"), lax.axis_index("ct")
    wide = parts[0].shape[2]
    half = lax.broadcasted_iota(jnp.int32, (1, wide), 1) < wide // 2
    straight = pair_bit(ct) == 1
    own_first = (tr & (3 - pair_bit(ct))) == 0
    copies = []
    for n, by_core in enumerate(shifts):
        shift = sum(jnp.where(ct == c, z, 0) for c, z in enumerate(by_core))
        at = pl.multiple_of(((tr // 4) ^ shift) * 2 * wide, 2 * wide)
        for i in range(out.shape[0]):
            a, b = parts[2 * n][i], parts[2 * n + 1][i]
            lo, hi = jnp.where(own_first, a, b), jnp.where(own_first, b, a)
            across = pltpu.roll(jnp.where(half, hi, lo).astype(F32), wide // 2, 1).astype(lo.dtype)
            stage[n, i, :, pl.ds(0, wide)] = jnp.where(straight, lo, jnp.where(half, lo, hi))
            stage[n, i, :, pl.ds(wide, wide)] = jnp.where(straight, hi, across)
        copies.append(pltpu.make_async_copy(stage.at[n], out.at[:, :, pl.ds(at, 2 * wide)], sems.at[n]))
        copies[-1].start()
    for copy in copies:
        copy.wait()


def per_device(n_tr, n_ct, amplitudes, cycle_integrals, pair_live):
    n_i, vt, n_k, cols = amplitudes.shape
    n_j = cycle_integrals.shape[2]
    n_local = n_i // n_ct
    n_z = n_tr // 4
    ct = lax.axis_index("ct")
    far = sorted(range(1, n_z), key=lambda z: -z)
    shared, split = far[: len(far) // n_ct * n_ct], far[len(far) // n_ct * n_ct :]
    groups = [shared[n : n + n_ct] for n in range(0, len(shared), n_ct)]
    shifts = [[group[c ^ e] for c in range(n_ct)] for group in groups for e in range(n_ct)]
    shifts += [[z] * n_ct for z in split] + [[0] * n_ct]

    def beside(c):
        return 3 - pair_bit(c)

    def over_ct(value, e):
        return lax.ppermute(value, "ct", [(c, c ^ e) for c in range(n_ct)])

    def over_tr(value, move, e=0):
        pairs = [(r * n_ct + c, (r ^ move(c ^ e)) * n_ct + (c ^ e)) for r in range(n_tr) for c in range(n_ct)]
        return lax.ppermute(value, ("tr", "ct"), pairs)

    def call(kernel, shape, inputs, after=(), gflop=0, dtype=jnp.bfloat16, count=None):
        result = jax.ShapeDtypeStruct(shape, dtype)
        return pl.pallas_call(
            kernel,
            out_shape=result if count is None else [result] * count,
            in_specs=[VMEM] * len(inputs) + [ANY] * len(after),
            out_specs=VMEM if count is None else [VMEM] * count,
            compiler_params=PARAMS,
            cost_estimate=cost(gflop),
        )(*inputs, *after)

    def pack(parts, after=(), gflop=0):
        shape = (sum(part.shape[0] for part in parts), *parts[0].shape[1:])
        return call(functools.partial(pack_kernel, len(parts)), shape, parts, after, gflop)

    own_w = jnp.transpose(cycle_integrals, (2, 0, 3, 1))
    masks = pl.pallas_call(
        functools.partial(masks_kernel, n_ct, n_k, n_local, vt),
        out_shape=jax.ShapeDtypeStruct((n_ct * n_k + n_local + 1, cols), F32),
        in_specs=[SMEM],
        out_specs=VMEM,
        compiler_params=PARAMS,
        cost_estimate=cost(),
    )(pair_live)

    by_group = jnp.transpose(amplitudes, (0, 2, 1, 3)).reshape(n_ct, n_local, n_k, vt, cols)
    given = [lax.dynamic_index_in_dim(by_group, ct ^ e, 0) for e in range(n_ct)]
    own_a = [given[0]] + [over_ct(given[e], e) for e in range(1, n_ct)]

    own_parts = pack([own_w] + [over_ct(own_w, e) for e in range(1, n_ct)], [given[0]])
    some = [over_tr(own_w, lambda c, z=z: 4 * z) for z in split]
    whole = [over_tr(own_parts, lambda c, group=group: 4 * group[c]) for group in groups]
    their_a = [over_tr(value, pair_bit, e) for e, value in enumerate(given)]
    whole = pack(whole, [masks, *some], 3)
    some = some[0] if len(some) == 1 else pack(some)
    whole_side = [over_tr(whole, beside, e) for e in range(n_ct)]
    whole_rest = [over_ct(whole, e) for e in range(1, n_ct)]
    some_rest = [over_ct(some, e) for e in range(1, n_ct)]
    some_side = over_tr(pack([own_parts, some, *some_rest], their_a), beside)

    n_some = some.shape[0]
    of_group = [[(n, g * n_ct + (e ^ n)) for e in range(n_ct)] for g in range(len(groups)) for n in range(n_ct)]
    column = of_group + [[(n_ct + e, n) for e in range(n_ct)] for n in range(len(split))]
    column += [[(2 * n_ct, e) for e in range(n_ct)]]
    side_near = [[(0, n_ct + e * n_some + n) for e in range(n_ct)] for n in range(len(split))]
    side_near += [[(0, e) for e in range(n_ct)]]

    def blocks(tiles, arrays, after, gflop):
        kernel = functools.partial(blocks_kernel, n_ct, tiles)
        inputs = [masks, *own_a, *their_a, *arrays]
        return call(kernel, (n_local, vt, 2 * vt), inputs, after, gflop, count=len(tiles))

    near = blocks(column, [whole, *whole_rest, some, *some_rest, own_parts], [], 0)
    made = near[:1]
    near = [over_tr(b, lambda c, by=by: 4 * by[c]) if any(by) else b for b, by in zip(near, shifts)]
    side = blocks(of_group, whole_side, made, 6)
    made = side[:1]
    side = [over_tr(b, lambda c, by=by: 4 * by[c] + beside(c)) for b, by in zip(side, shifts)]
    late = blocks(side_near, [some_side], [*made, *near[:2]], 3)
    done = call(join_kernel, (8, 128), [], side, 10, F32)
    side += [over_tr(b, lambda c, by=by: 4 * by[c] + beside(c)) for b, by in zip(late, shifts[len(shared) :])]

    moved = [block for both in zip(near, side) for block in both]
    result = pl.pallas_call(
        functools.partial(place_kernel, shifts),
        out_shape=jax.ShapeDtypeStruct((n_local, vt, n_tr * vt), jnp.bfloat16),
        in_specs=[VMEM] * len(moved) + [ANY],
        out_specs=ANY,
        scratch_shapes=[
            pltpu.VMEM((n_z, n_local, vt, 4 * vt), jnp.bfloat16),
            pltpu.SemaphoreType.DMA((n_z,)),
        ],
        compiler_params=PARAMS,
        cost_estimate=cost(),
    )(*moved, done)
    return result.reshape(n_local, vt, n_j, n_tr * vt)


def solution(mesh):
    return jax.shard_map(
        functools.partial(per_device, mesh.shape["tr"], mesh.shape["ct"]),
        mesh=mesh,
        in_specs=(P(None, "tr", None, "ct"), P(None, "ct", None, "tr"), P()),
        out_specs=P("ct", "tr", None, None),
        check_vma=False,
    )
```

```python
import functools

import jax
import jax.numpy as jnp
from jax import lax
from jax.experimental import pallas as pl
from jax.experimental.pallas import tpu as pltpu
from jax.sharding import PartitionSpec as P

F32 = jnp.float32
VMEM = pl.BlockSpec(memory_space=pltpu.VMEM)
ANY = pl.BlockSpec(memory_space=pl.ANY)
SMEM = pl.BlockSpec(memory_space=pltpu.SMEM)
PARAMS = pltpu.CompilerParams(vmem_limit_bytes=16 * 1024 * 1024)


def cost(gflop=0):
    return pl.CostEstimate(flops=1 + gflop * 1_000_000_000, bytes_accessed=1, transcendentals=0)


def pair_bit(ct):
    return 1 + ct % 2


def masks_kernel(n_ct, n_k, n_local, vt, live, out):
    tr, ct = lax.axis_index("tr"), lax.axis_index("ct")
    cols = out.shape[1]
    bit = pair_bit(ct)
    turned = (bit == 2) & ((tr & 1) == 1)
    members = [(tr & ~bit) + jnp.where(turned, bit, 0), (tr & ~bit) + jnp.where(turned, 0, bit)]
    tile = lax.broadcasted_iota(jnp.int32, (1, cols), 1) // vt
    for e in range(n_ct):
        for k in range(n_k):
            mask = jnp.zeros((1, cols), F32)
            for t in range(cols // vt):
                mask = jnp.where(tile == t, live[k, (ct ^ e) * (cols // vt) + t].astype(F32), mask)
            out[pl.ds(e * n_k + k, 1)] = mask
    for i in range(n_local):
        row = ct * n_local + i
        both = jnp.where(tile < 1, live[row, members[0]].astype(F32), live[row, members[1]].astype(F32))
        out[pl.ds(n_ct * n_k + i, 1)] = both
    out[pl.ds(n_ct * n_k + n_local, 1)] = jnp.full((1, cols), (members[0] == tr).astype(F32))


def pack_kernel(count, *refs):
    out, at = refs[-1], 0
    for ref in refs[:count]:
        out[pl.ds(at, ref.shape[0])] = ref[...]
        at += ref.shape[0]


def blocks_kernel(n_ct, tiles_at, masks, *refs):
    own, theirs, arrays, outs = refs[:n_ct], refs[n_ct : 2 * n_ct], refs[2 * n_ct :], refs[-len(tiles_at) :]
    n_local, n_k, vt, cols = own[0].shape[1:]
    first = masks[pl.ds(n_ct * n_k + n_local, 1)] > 0
    lhs = {}
    for e in range(n_ct):
        for k in range(n_k):
            stacked = jnp.concatenate([arrays[n][at, k] for n, at in (tile[e] for tile in tiles_at)], axis=0)
            lhs[e, k] = stacked * masks[pl.ds(e * n_k + k, 1)].astype(jnp.bfloat16)
    step = min(2, n_local)
    for start in range(0, n_local, step):
        total = None
        for (e, k), left in lhs.items():
            rows = []
            for i in range(start, start + step):
                a, b = own[e][0, i, k], theirs[e][0, i, k]
                rows += [jnp.where(first, a, b), jnp.where(first, b, a)]
            term = lax.dot_general(
                left,
                jnp.concatenate(rows, axis=0),
                (((1,), (1,)), ((), ())),
                preferred_element_type=F32,
            )
            total = term if total is None else total + term
        for i in range(start, start + step):
            row_mask = masks[pl.ds(n_ct * n_k + i, 1), pl.ds(0, 2 * vt)]
            kept = total[:, (i - start) * 2 * vt : (i - start + 1) * 2 * vt] * row_mask
            for d, out in enumerate(outs):
                out[i] = kept[d * vt : (d + 1) * vt].astype(out.dtype)


def join_kernel(*refs):
    refs[-1][...] = jnp.zeros_like(refs[-1])


def place_kernel(shifts, *refs):
    parts, (out, stage, sems) = refs, refs[-3:]
    tr, ct = lax.axis_index("tr"), lax.axis_index("ct")
    wide = parts[0].shape[2]
    half = lax.broadcasted_iota(jnp.int32, (1, wide), 1) < wide // 2
    straight = pair_bit(ct) == 1
    own_first = (tr & (3 - pair_bit(ct))) == 0
    copies = []
    for n, by_core in enumerate(shifts):
        shift = sum(jnp.where(ct == c, z, 0) for c, z in enumerate(by_core))
        at = pl.multiple_of(((tr // 4) ^ shift) * 2 * wide, 2 * wide)
        for i in range(out.shape[0]):
            a, b = parts[2 * n][i], parts[2 * n + 1][i]
            lo, hi = jnp.where(own_first, a, b), jnp.where(own_first, b, a)
            across = pltpu.roll(jnp.where(half, hi, lo).astype(F32), wide // 2, 1).astype(lo.dtype)
            stage[n, i, :, pl.ds(0, wide)] = jnp.where(straight, lo, jnp.where(half, lo, hi))
            stage[n, i, :, pl.ds(wide, wide)] = jnp.where(straight, hi, across)
        copies.append(pltpu.make_async_copy(stage.at[n], out.at[:, :, pl.ds(at, 2 * wide)], sems.at[n]))
        copies[-1].start()
    for copy in copies:
        copy.wait()


def per_device(n_tr, n_ct, amplitudes, cycle_integrals, pair_live):
    n_i, vt, n_k, cols = amplitudes.shape
    n_j = cycle_integrals.shape[2]
    n_local = n_i // n_ct
    n_z = n_tr // 4
    ct = lax.axis_index("ct")
    far = sorted(range(1, n_z), key=lambda z: -z)
    shared, split = far[: len(far) // n_ct * n_ct], far[len(far) // n_ct * n_ct :]
    groups = [shared[n : n + n_ct] for n in range(0, len(shared), n_ct)]
    shifts = [[group[c ^ e] for c in range(n_ct)] for group in groups for e in range(n_ct)]
    shifts += [[z] * n_ct for z in split] + [[0] * n_ct]

    def beside(c):
        return 3 - pair_bit(c)

    def over_ct(value, e):
        return lax.ppermute(value, "ct", [(c, c ^ e) for c in range(n_ct)])

    def over_tr(value, move, e=0):
        pairs = [(r * n_ct + c, (r ^ move(c ^ e)) * n_ct + (c ^ e)) for r in range(n_tr) for c in range(n_ct)]
        return lax.ppermute(value, ("tr", "ct"), pairs)

    def call(kernel, shape, inputs, after=(), gflop=0, dtype=jnp.bfloat16, count=None):
        result = jax.ShapeDtypeStruct(shape, dtype)
        return pl.pallas_call(
            kernel,
            out_shape=result if count is None else [result] * count,
            in_specs=[VMEM] * len(inputs) + [ANY] * len(after),
            out_specs=VMEM if count is None else [VMEM] * count,
            compiler_params=PARAMS,
            cost_estimate=cost(gflop),
        )(*inputs, *after)

    def pack(parts, after=(), gflop=0):
        shape = (sum(part.shape[0] for part in parts), *parts[0].shape[1:])
        return call(functools.partial(pack_kernel, len(parts)), shape, parts, after, gflop)

    own_w = jnp.transpose(cycle_integrals, (2, 0, 3, 1))
    masks = pl.pallas_call(
        functools.partial(masks_kernel, n_ct, n_k, n_local, vt),
        out_shape=jax.ShapeDtypeStruct((n_ct * n_k + n_local + 1, cols), F32),
        in_specs=[SMEM],
        out_specs=VMEM,
        compiler_params=PARAMS,
        cost_estimate=cost(),
    )(pair_live)

    by_group = jnp.transpose(amplitudes, (0, 2, 1, 3)).reshape(n_ct, n_local, n_k, vt, cols)
    given = [lax.dynamic_index_in_dim(by_group, ct ^ e, 0) for e in range(n_ct)]
    own_a = [given[0]] + [over_ct(given[e], e) for e in range(1, n_ct)]

    own_parts = pack([own_w] + [over_ct(own_w, e) for e in range(1, n_ct)])
    some = [over_tr(own_w, lambda c, z=z: 4 * z) for z in split]
    whole = [over_tr(own_parts, lambda c, group=group: 4 * group[c]) for group in groups]
    their_a = [over_tr(value, pair_bit, e) for e, value in enumerate(given)]
    whole = pack(whole, [masks, *some], 3)
    some = some[0] if len(some) == 1 else pack(some)
    whole_side = [over_tr(whole, beside, e) for e in range(n_ct)]
    whole_rest = [over_ct(whole, e) for e in range(1, n_ct)]
    some_rest = [over_ct(some, e) for e in range(1, n_ct)]
    some_side = over_tr(pack([own_parts, some, *some_rest], their_a[:1]), beside)

    n_some = some.shape[0]
    of_group = [[(n, g * n_ct + (e ^ n)) for e in range(n_ct)] for g in range(len(groups)) for n in range(n_ct)]
    column = of_group + [[(n_ct + e, n) for e in range(n_ct)] for n in range(len(split))]
    column += [[(2 * n_ct, e) for e in range(n_ct)]]
    side_near = [[(0, n_ct + e * n_some + n) for e in range(n_ct)] for n in range(len(split))]
    side_near += [[(0, e) for e in range(n_ct)]]

    def blocks(tiles, arrays, after, gflop):
        kernel = functools.partial(blocks_kernel, n_ct, tiles)
        inputs = [masks, *own_a, *their_a, *arrays]
        return call(kernel, (n_local, vt, 2 * vt), inputs, after, gflop, count=len(tiles))

    near = blocks(column, [whole, *whole_rest, some, *some_rest, own_parts], [], 0)
    made = near[:1]
    near = [over_tr(b, lambda c, by=by: 4 * by[c]) if any(by) else b for b, by in zip(near, shifts)]
    side = blocks(of_group, whole_side, made, 6)
    made = side[:1]
    side = [over_tr(b, lambda c, by=by: 4 * by[c] + beside(c)) for b, by in zip(side, shifts)]
    late = blocks(side_near, [some_side], [*made, *near[:2]], 3)
    done = call(join_kernel, (8, 128), [], side, 10, F32)
    side += [over_tr(b, lambda c, by=by: 4 * by[c] + beside(c)) for b, by in zip(late, shifts[len(shared) :])]

    moved = [block for both in zip(near, side) for block in both]
    result = pl.pallas_call(
        functools.partial(place_kernel, shifts),
        out_shape=jax.ShapeDtypeStruct((n_local, vt, n_tr * vt), jnp.bfloat16),
        in_specs=[VMEM] * len(moved) + [ANY],
        out_specs=ANY,
        scratch_shapes=[
            pltpu.VMEM((n_z, n_local, vt, 4 * vt), jnp.bfloat16),
            pltpu.SemaphoreType.DMA((n_z,)),
        ],
        compiler_params=PARAMS,
        cost_estimate=cost(),
    )(*moved, done)
    return result.reshape(n_local, vt, n_j, n_tr * vt)


def solution(mesh):
    return jax.shard_map(
        functools.partial(per_device, mesh.shape["tr"], mesh.shape["ct"]),
        mesh=mesh,
        in_specs=(P(None, "tr", None, "ct"), P(None, "ct", None, "tr"), P()),
        out_specs=P("ct", "tr", None, None),
        check_vma=False,
    )
```

```python
import functools

import jax
import jax.numpy as jnp
from jax import lax
from jax.experimental import pallas as pl
from jax.experimental.pallas import tpu as pltpu
from jax.sharding import PartitionSpec as P

F32 = jnp.float32
VMEM = pl.BlockSpec(memory_space=pltpu.VMEM)
ANY = pl.BlockSpec(memory_space=pl.ANY)
SMEM = pl.BlockSpec(memory_space=pltpu.SMEM)
PARAMS = pltpu.CompilerParams(vmem_limit_bytes=16 * 1024 * 1024)


def cost(gflop=0):
    return pl.CostEstimate(flops=1 + gflop * 1_000_000_000, bytes_accessed=1, transcendentals=0)


def pair_bit(ct):
    return 1 + ct % 2


def masks_kernel(n_ct, n_k, n_local, vt, live, out):
    tr, ct = lax.axis_index("tr"), lax.axis_index("ct")
    cols = out.shape[1]
    bit = pair_bit(ct)
    turned = (bit == 2) & ((tr & 1) == 1)
    members = [(tr & ~bit) + jnp.where(turned, bit, 0), (tr & ~bit) + jnp.where(turned, 0, bit)]
    tile = lax.broadcasted_iota(jnp.int32, (1, cols), 1) // vt
    for e in range(n_ct):
        for k in range(n_k):
            mask = jnp.zeros((1, cols), F32)
            for t in range(cols // vt):
                mask = jnp.where(tile == t, live[k, (ct ^ e) * (cols // vt) + t].astype(F32), mask)
            out[pl.ds(e * n_k + k, 1)] = mask
    for i in range(n_local):
        row = ct * n_local + i
        both = jnp.where(tile < 1, live[row, members[0]].astype(F32), live[row, members[1]].astype(F32))
        out[pl.ds(n_ct * n_k + i, 1)] = both
    out[pl.ds(n_ct * n_k + n_local, 1)] = jnp.full((1, cols), (members[0] == tr).astype(F32))


def pack_kernel(count, *refs):
    out, at = refs[-1], 0
    for ref in refs[:count]:
        out[pl.ds(at, ref.shape[0])] = ref[...]
        at += ref.shape[0]


def blocks_kernel(n_ct, tiles_at, masks, *refs):
    own, theirs, arrays, outs = refs[:n_ct], refs[n_ct : 2 * n_ct], refs[2 * n_ct :], refs[-len(tiles_at) :]
    n_local, n_k, vt, cols = own[0].shape[1:]
    first = masks[pl.ds(n_ct * n_k + n_local, 1)] > 0
    lhs = {}
    for e in range(n_ct):
        for k in range(n_k):
            stacked = jnp.concatenate([arrays[n][at, k] for n, at in (tile[e] for tile in tiles_at)], axis=0)
            lhs[e, k] = stacked * masks[pl.ds(e * n_k + k, 1)].astype(jnp.bfloat16)
    step = min(2, n_local)
    for start in range(0, n_local, step):
        total = None
        for (e, k), left in lhs.items():
            rows = []
            for i in range(start, start + step):
                a, b = own[e][0, i, k], theirs[e][0, i, k]
                rows += [jnp.where(first, a, b), jnp.where(first, b, a)]
            term = lax.dot_general(
                left,
                jnp.concatenate(rows, axis=0),
                (((1,), (1,)), ((), ())),
                preferred_element_type=F32,
            )
            total = term if total is None else total + term
        for i in range(start, start + step):
            row_mask = masks[pl.ds(n_ct * n_k + i, 1), pl.ds(0, 2 * vt)]
            kept = total[:, (i - start) * 2 * vt : (i - start + 1) * 2 * vt] * row_mask
            for d, out in enumerate(outs):
                out[i] = kept[d * vt : (d + 1) * vt].astype(out.dtype)


def join_kernel(*refs):
    refs[-1][...] = jnp.zeros_like(refs[-1])


def place_kernel(shifts, *refs):
    parts, (out, stage, sems) = refs, refs[-3:]
    tr, ct = lax.axis_index("tr"), lax.axis_index("ct")
    wide = parts[0].shape[2]
    half = lax.broadcasted_iota(jnp.int32, (1, wide), 1) < wide // 2
    straight = pair_bit(ct) == 1
    own_first = (tr & (3 - pair_bit(ct))) == 0
    copies = []
    for n, by_core in enumerate(shifts):
        shift = sum(jnp.where(ct == c, z, 0) for c, z in enumerate(by_core))
        at = pl.multiple_of(((tr // 4) ^ shift) * 2 * wide, 2 * wide)
        for i in range(out.shape[0]):
            a, b = parts[2 * n][i], parts[2 * n + 1][i]
            lo, hi = jnp.where(own_first, a, b), jnp.where(own_first, b, a)
            across = pltpu.roll(jnp.where(half, hi, lo).astype(F32), wide // 2, 1).astype(lo.dtype)
            stage[n, i, :, pl.ds(0, wide)] = jnp.where(straight, lo, jnp.where(half, lo, hi))
            stage[n, i, :, pl.ds(wide, wide)] = jnp.where(straight, hi, across)
        copies.append(pltpu.make_async_copy(stage.at[n], out.at[:, :, pl.ds(at, 2 * wide)], sems.at[n]))
        copies[-1].start()
    for copy in copies:
        copy.wait()


def per_device(n_tr, n_ct, amplitudes, cycle_integrals, pair_live):
    n_i, vt, n_k, cols = amplitudes.shape
    n_j = cycle_integrals.shape[2]
    n_local = n_i // n_ct
    n_z = n_tr // 4
    ct = lax.axis_index("ct")
    far = sorted(range(1, n_z), key=lambda z: -z)
    shared, split = far[: len(far) // n_ct * n_ct], far[len(far) // n_ct * n_ct :]
    groups = [shared[n : n + n_ct] for n in range(0, len(shared), n_ct)]
    shifts = [[group[c ^ e] for c in range(n_ct)] for group in groups for e in range(n_ct)]
    shifts += [[z] * n_ct for z in split] + [[0] * n_ct]

    def beside(c):
        return 3 - pair_bit(c)

    def over_ct(value, e):
        return lax.ppermute(value, "ct", [(c, c ^ e) for c in range(n_ct)])

    def over_tr(value, move, e=0):
        pairs = [(r * n_ct + c, (r ^ move(c ^ e)) * n_ct + (c ^ e)) for r in range(n_tr) for c in range(n_ct)]
        return lax.ppermute(value, ("tr", "ct"), pairs)

    def call(kernel, shape, inputs, after=(), gflop=0, dtype=jnp.bfloat16, count=None):
        result = jax.ShapeDtypeStruct(shape, dtype)
        return pl.pallas_call(
            kernel,
            out_shape=result if count is None else [result] * count,
            in_specs=[VMEM] * len(inputs) + [ANY] * len(after),
            out_specs=VMEM if count is None else [VMEM] * count,
            compiler_params=PARAMS,
            cost_estimate=cost(gflop),
        )(*inputs, *after)

    def pack(parts, after=(), gflop=0):
        shape = (sum(part.shape[0] for part in parts), *parts[0].shape[1:])
        return call(functools.partial(pack_kernel, len(parts)), shape, parts, after, gflop)

    own_w = jnp.transpose(cycle_integrals, (2, 0, 3, 1))
    masks = pl.pallas_call(
        functools.partial(masks_kernel, n_ct, n_k, n_local, vt),
        out_shape=jax.ShapeDtypeStruct((n_ct * n_k + n_local + 1, cols), F32),
        in_specs=[SMEM],
        out_specs=VMEM,
        compiler_params=PARAMS,
        cost_estimate=cost(),
    )(pair_live)

    by_group = jnp.transpose(amplitudes, (0, 2, 1, 3)).reshape(n_ct, n_local, n_k, vt, cols)
    given = [lax.dynamic_index_in_dim(by_group, ct ^ e, 0) for e in range(n_ct)]
    own_a = [given[0]] + [over_ct(given[e], e) for e in range(1, n_ct)]

    own_parts = pack([own_w] + [over_ct(own_w, e) for e in range(1, n_ct)])
    some = [over_tr(own_w, lambda c, z=z: 4 * z) for z in split]
    whole = [over_tr(own_parts, lambda c, group=group: 4 * group[c]) for group in groups]
    their_a = [over_tr(value, pair_bit, e) for e, value in enumerate(given)]
    whole = pack(whole, [masks, *some], 3)
    some = some[0] if len(some) == 1 else pack(some)
    whole_side = [over_tr(whole, beside, e) for e in range(n_ct)]
    whole_rest = [over_ct(whole, e) for e in range(1, n_ct)]
    some_rest = [over_ct(some, e) for e in range(1, n_ct)]
    some_side = over_tr(pack([own_parts, some, *some_rest], their_a[1:]), beside)

    n_some = some.shape[0]
    of_group = [[(n, g * n_ct + (e ^ n)) for e in range(n_ct)] for g in range(len(groups)) for n in range(n_ct)]
    column = of_group + [[(n_ct + e, n) for e in range(n_ct)] for n in range(len(split))]
    column += [[(2 * n_ct, e) for e in range(n_ct)]]
    side_near = [[(0, n_ct + e * n_some + n) for e in range(n_ct)] for n in range(len(split))]
    side_near += [[(0, e) for e in range(n_ct)]]

    def blocks(tiles, arrays, after, gflop):
        kernel = functools.partial(blocks_kernel, n_ct, tiles)
        inputs = [masks, *own_a, *their_a, *arrays]
        return call(kernel, (n_local, vt, 2 * vt), inputs, after, gflop, count=len(tiles))

    near = blocks(column, [whole, *whole_rest, some, *some_rest, own_parts], [], 0)
    made = near[:1]
    near = [over_tr(b, lambda c, by=by: 4 * by[c]) if any(by) else b for b, by in zip(near, shifts)]
    side = blocks(of_group, whole_side, made, 9)
    made = side[:1]
    side = [over_tr(b, lambda c, by=by: 4 * by[c] + beside(c)) for b, by in zip(side, shifts)]
    late = blocks(side_near, [some_side], [*made, *near[:2]], 8)
    done = call(join_kernel, (8, 128), [], side, 10, F32)
    side += [over_tr(b, lambda c, by=by: 4 * by[c] + beside(c)) for b, by in zip(late, shifts[len(shared) :])]

    moved = [block for both in zip(near, side) for block in both]
    result = pl.pallas_call(
        functools.partial(place_kernel, shifts),
        out_shape=jax.ShapeDtypeStruct((n_local, vt, n_tr * vt), jnp.bfloat16),
        in_specs=[VMEM] * len(moved) + [ANY],
        out_specs=ANY,
        scratch_shapes=[
            pltpu.VMEM((n_z, n_local, vt, 4 * vt), jnp.bfloat16),
            pltpu.SemaphoreType.DMA((n_z,)),
        ],
        compiler_params=PARAMS,
        cost_estimate=cost(),
    )(*moved, done)
    return result.reshape(n_local, vt, n_j, n_tr * vt)


def solution(mesh):
    return jax.shard_map(
        functools.partial(per_device, mesh.shape["tr"], mesh.shape["ct"]),
        mesh=mesh,
        in_specs=(P(None, "tr", None, "ct"), P(None, "ct", None, "tr"), P()),
        out_specs=P("ct", "tr", None, None),
        check_vma=False,
    )
```

```python
import functools

import jax
import jax.numpy as jnp
from jax import lax
from jax.experimental import pallas as pl
from jax.experimental.pallas import tpu as pltpu
from jax.sharding import PartitionSpec as P

F32 = jnp.float32
VMEM = pl.BlockSpec(memory_space=pltpu.VMEM)
ANY = pl.BlockSpec(memory_space=pl.ANY)
SMEM = pl.BlockSpec(memory_space=pltpu.SMEM)
PARAMS = pltpu.CompilerParams(vmem_limit_bytes=16 * 1024 * 1024)


def cost(gflop=0):
    return pl.CostEstimate(flops=1 + gflop * 1_000_000_000, bytes_accessed=1, transcendentals=0)


def pair_bit(ct):
    return 1 + ct % 2


def masks_kernel(n_ct, n_k, n_local, vt, live, out):
    tr, ct = lax.axis_index("tr"), lax.axis_index("ct")
    cols = out.shape[1]
    bit = pair_bit(ct)
    turned = (bit == 2) & ((tr & 1) == 1)
    members = [(tr & ~bit) + jnp.where(turned, bit, 0), (tr & ~bit) + jnp.where(turned, 0, bit)]
    tile = lax.broadcasted_iota(jnp.int32, (1, cols), 1) // vt
    for e in range(n_ct):
        for k in range(n_k):
            mask = jnp.zeros((1, cols), F32)
            for t in range(cols // vt):
                mask = jnp.where(tile == t, live[k, (ct ^ e) * (cols // vt) + t].astype(F32), mask)
            out[pl.ds(e * n_k + k, 1)] = mask
    for i in range(n_local):
        row = ct * n_local + i
        both = jnp.where(tile < 1, live[row, members[0]].astype(F32), live[row, members[1]].astype(F32))
        out[pl.ds(n_ct * n_k + i, 1)] = both
    out[pl.ds(n_ct * n_k + n_local, 1)] = jnp.full((1, cols), (members[0] == tr).astype(F32))


def pack_kernel(count, *refs):
    out, at = refs[-1], 0
    for ref in refs[:count]:
        out[pl.ds(at, ref.shape[0])] = ref[...]
        at += ref.shape[0]


def blocks_kernel(n_ct, tiles_at, masks, *refs):
    own, theirs, arrays, outs = refs[:n_ct], refs[n_ct : 2 * n_ct], refs[2 * n_ct :], refs[-len(tiles_at) :]
    n_local, n_k, vt, cols = own[0].shape[1:]
    first = masks[pl.ds(n_ct * n_k + n_local, 1)] > 0
    lhs = {}
    for e in range(n_ct):
        for k in range(n_k):
            stacked = jnp.concatenate([arrays[n][at, k] for n, at in (tile[e] for tile in tiles_at)], axis=0)
            lhs[e, k] = stacked * masks[pl.ds(e * n_k + k, 1)].astype(jnp.bfloat16)
    step = min(2, n_local)
    for start in range(0, n_local, step):
        total = None
        for (e, k), left in lhs.items():
            rows = []
            for i in range(start, start + step):
                a, b = own[e][0, i, k], theirs[e][0, i, k]
                rows += [jnp.where(first, a, b), jnp.where(first, b, a)]
            term = lax.dot_general(
                left,
                jnp.concatenate(rows, axis=0),
                (((1,), (1,)), ((), ())),
                preferred_element_type=F32,
            )
            total = term if total is None else total + term
        for i in range(start, start + step):
            row_mask = masks[pl.ds(n_ct * n_k + i, 1), pl.ds(0, 2 * vt)]
            kept = total[:, (i - start) * 2 * vt : (i - start + 1) * 2 * vt] * row_mask
            for d, out in enumerate(outs):
                out[i] = kept[d * vt : (d + 1) * vt].astype(out.dtype)


def join_kernel(*refs):
    refs[-1][...] = jnp.zeros_like(refs[-1])


def place_kernel(shifts, *refs):
    parts, (out, stage, sems) = refs, refs[-3:]
    tr, ct = lax.axis_index("tr"), lax.axis_index("ct")
    wide = parts[0].shape[2]
    half = lax.broadcasted_iota(jnp.int32, (1, wide), 1) < wide // 2
    straight = pair_bit(ct) == 1
    own_first = (tr & (3 - pair_bit(ct))) == 0
    places = []
    for by_core in shifts:
        shift = sum(jnp.where(ct == c, z, 0) for c, z in enumerate(by_core))
        places.append(pl.multiple_of(((tr // 4) ^ shift) * 2 * wide, 2 * wide))

    @pl.when(straight)
    def _():
        copies = []
        for n, at in enumerate(places):
            for m in range(2):
                lane = pl.multiple_of(at + jnp.where(own_first, m, 1 - m) * wide, wide)
                copies.append(
                    pltpu.make_async_copy(parts[2 * n + m], out.at[:, :, pl.ds(lane, wide)], sems.at[2 * n + m])
                )
                copies[-1].start()
        for copy in copies:
            copy.wait()

    @pl.when(jnp.logical_not(straight))
    def _():
        copies = []
        for n, at in enumerate(places):
            for i in range(out.shape[0]):
                a, b = parts[2 * n][i], parts[2 * n + 1][i]
                lo, hi = jnp.where(own_first, a, b), jnp.where(own_first, b, a)
                across = pltpu.roll(jnp.where(half, hi, lo).astype(F32), wide // 2, 1).astype(lo.dtype)
                stage[n, i, :, pl.ds(0, wide)] = jnp.where(half, lo, hi)
                stage[n, i, :, pl.ds(wide, wide)] = across
            copies.append(pltpu.make_async_copy(stage.at[n], out.at[:, :, pl.ds(at, 2 * wide)], sems.at[2 * n]))
            copies[-1].start()
        for copy in copies:
            copy.wait()


def per_device(n_tr, n_ct, amplitudes, cycle_integrals, pair_live):
    n_i, vt, n_k, cols = amplitudes.shape
    n_j = cycle_integrals.shape[2]
    n_local = n_i // n_ct
    n_z = n_tr // 4
    ct = lax.axis_index("ct")
    far = sorted(range(1, n_z), key=lambda z: -z)
    shared, split = far[: len(far) // n_ct * n_ct], far[len(far) // n_ct * n_ct :]
    groups = [shared[n : n + n_ct] for n in range(0, len(shared), n_ct)]
    shifts = [[group[c ^ e] for c in range(n_ct)] for group in groups for e in range(n_ct)]
    shifts += [[z] * n_ct for z in split] + [[0] * n_ct]

    def beside(c):
        return 3 - pair_bit(c)

    def over_ct(value, e):
        return lax.ppermute(value, "ct", [(c, c ^ e) for c in range(n_ct)])

    def over_tr(value, move, e=0):
        pairs = [(r * n_ct + c, (r ^ move(c ^ e)) * n_ct + (c ^ e)) for r in range(n_tr) for c in range(n_ct)]
        return lax.ppermute(value, ("tr", "ct"), pairs)

    def call(kernel, shape, inputs, after=(), gflop=0, dtype=jnp.bfloat16, count=None):
        result = jax.ShapeDtypeStruct(shape, dtype)
        return pl.pallas_call(
            kernel,
            out_shape=result if count is None else [result] * count,
            in_specs=[VMEM] * len(inputs) + [ANY] * len(after),
            out_specs=VMEM if count is None else [VMEM] * count,
            compiler_params=PARAMS,
            cost_estimate=cost(gflop),
        )(*inputs, *after)

    def pack(parts, after=(), gflop=0):
        shape = (sum(part.shape[0] for part in parts), *parts[0].shape[1:])
        return call(functools.partial(pack_kernel, len(parts)), shape, parts, after, gflop)

    own_w = jnp.transpose(cycle_integrals, (2, 0, 3, 1))
    masks = pl.pallas_call(
        functools.partial(masks_kernel, n_ct, n_k, n_local, vt),
        out_shape=jax.ShapeDtypeStruct((n_ct * n_k + n_local + 1, cols), F32),
        in_specs=[SMEM],
        out_specs=VMEM,
        compiler_params=PARAMS,
        cost_estimate=cost(),
    )(pair_live)

    by_group = jnp.transpose(amplitudes, (0, 2, 1, 3)).reshape(n_ct, n_local, n_k, vt, cols)
    given = [lax.dynamic_index_in_dim(by_group, ct ^ e, 0) for e in range(n_ct)]
    own_a = [given[0]] + [over_ct(given[e], e) for e in range(1, n_ct)]

    own_parts = pack([own_w] + [over_ct(own_w, e) for e in range(1, n_ct)])
    some = [over_tr(own_w, lambda c, z=z: 4 * z) for z in split]
    whole = [over_tr(own_parts, lambda c, group=group: 4 * group[c]) for group in groups]
    their_a = [over_tr(value, pair_bit, e) for e, value in enumerate(given)]
    whole = pack(whole, [masks, *some], 3)
    some = some[0] if len(some) == 1 else pack(some)
    whole_side = [over_tr(whole, beside, e) for e in range(n_ct)]
    whole_rest = [over_ct(whole, e) for e in range(1, n_ct)]
    some_rest = [over_ct(some, e) for e in range(1, n_ct)]
    some_side = over_tr(pack([own_parts, some, *some_rest], their_a[1:]), beside)

    n_some = some.shape[0]
    of_group = [[(n, g * n_ct + (e ^ n)) for e in range(n_ct)] for g in range(len(groups)) for n in range(n_ct)]
    column = of_group + [[(n_ct + e, n) for e in range(n_ct)] for n in range(len(split))]
    column += [[(2 * n_ct, e) for e in range(n_ct)]]
    side_near = [[(0, n_ct + e * n_some + n) for e in range(n_ct)] for n in range(len(split))]
    side_near += [[(0, e) for e in range(n_ct)]]

    def blocks(tiles, arrays, after, gflop):
        kernel = functools.partial(blocks_kernel, n_ct, tiles)
        inputs = [masks, *own_a, *their_a, *arrays]
        return call(kernel, (n_local, vt, 2 * vt), inputs, after, gflop, count=len(tiles))

    near = blocks(column, [whole, *whole_rest, some, *some_rest, own_parts], [], 0)
    made = near[:1]
    near = [over_tr(b, lambda c, by=by: 4 * by[c]) if any(by) else b for b, by in zip(near, shifts)]
    side = blocks(of_group, whole_side, made, 9)
    made = side[:1]
    side = [over_tr(b, lambda c, by=by: 4 * by[c] + beside(c)) for b, by in zip(side, shifts)]
    late = blocks(side_near, [some_side], [*made, *near[:2]], 8)
    done = call(join_kernel, (8, 128), [], side, 10, F32)
    side += [over_tr(b, lambda c, by=by: 4 * by[c] + beside(c)) for b, by in zip(late, shifts[len(shared) :])]

    moved = [block for both in zip(near, side) for block in both]
    result = pl.pallas_call(
        functools.partial(place_kernel, shifts),
        out_shape=jax.ShapeDtypeStruct((n_local, vt, n_tr * vt), jnp.bfloat16),
        in_specs=[VMEM] * len(moved) + [ANY],
        out_specs=ANY,
        scratch_shapes=[
            pltpu.VMEM((n_z, n_local, vt, 4 * vt), jnp.bfloat16),
            pltpu.SemaphoreType.DMA((2 * n_z,)),
        ],
        compiler_params=PARAMS,
        cost_estimate=cost(),
    )(*moved, done)
    return result.reshape(n_local, vt, n_j, n_tr * vt)


def solution(mesh):
    return jax.shard_map(
        functools.partial(per_device, mesh.shape["tr"], mesh.shape["ct"]),
        mesh=mesh,
        in_specs=(P(None, "tr", None, "ct"), P(None, "ct", None, "tr"), P()),
        out_specs=P("ct", "tr", None, None),
        check_vma=False,
    )
```

```python
import functools

import jax
import jax.numpy as jnp
from jax import lax
from jax.experimental import pallas as pl
from jax.experimental.pallas import tpu as pltpu
from jax.sharding import PartitionSpec as P

F32 = jnp.float32
VMEM = pl.BlockSpec(memory_space=pltpu.VMEM)
ANY = pl.BlockSpec(memory_space=pl.ANY)
SMEM = pl.BlockSpec(memory_space=pltpu.SMEM)
PARAMS = pltpu.CompilerParams(vmem_limit_bytes=16 * 1024 * 1024)


def cost(gflop=0):
    return pl.CostEstimate(flops=1 + gflop * 1_000_000_000, bytes_accessed=1, transcendentals=0)


def pair_bit(ct):
    return 1 + ct % 2


def masks_kernel(n_ct, n_k, n_local, vt, live, out):
    tr, ct = lax.axis_index("tr"), lax.axis_index("ct")
    cols = out.shape[1]
    bit = pair_bit(ct)
    turned = (bit == 2) & ((tr & 1) == 1)
    members = [(tr & ~bit) + jnp.where(turned, bit, 0), (tr & ~bit) + jnp.where(turned, 0, bit)]
    tile = lax.broadcasted_iota(jnp.int32, (1, cols), 1) // vt
    for e in range(n_ct):
        for k in range(n_k):
            mask = jnp.zeros((1, cols), F32)
            for t in range(cols // vt):
                mask = jnp.where(tile == t, live[k, (ct ^ e) * (cols // vt) + t].astype(F32), mask)
            out[pl.ds(e * n_k + k, 1)] = mask
    for i in range(n_local):
        row = ct * n_local + i
        both = jnp.where(tile < 1, live[row, members[0]].astype(F32), live[row, members[1]].astype(F32))
        out[pl.ds(n_ct * n_k + i, 1)] = both
    out[pl.ds(n_ct * n_k + n_local, 1)] = jnp.full((1, cols), (members[0] == tr).astype(F32))


def pack_kernel(count, *refs):
    out, at = refs[-1], 0
    for ref in refs[:count]:
        out[pl.ds(at, ref.shape[0])] = ref[...]
        at += ref.shape[0]


def blocks_kernel(n_ct, tiles_at, masks, *refs):
    own, theirs, arrays, outs = refs[:n_ct], refs[n_ct : 2 * n_ct], refs[2 * n_ct :], refs[-len(tiles_at) :]
    n_local, n_k, vt, cols = own[0].shape[1:]
    first = masks[pl.ds(n_ct * n_k + n_local, 1)] > 0
    lhs = {}
    for e in range(n_ct):
        for k in range(n_k):
            stacked = jnp.concatenate([arrays[n][at, k] for n, at in (tile[e] for tile in tiles_at)], axis=0)
            lhs[e, k] = stacked * masks[pl.ds(e * n_k + k, 1)].astype(jnp.bfloat16)
    step = min(2, n_local)
    for start in range(0, n_local, step):
        total = None
        for (e, k), left in lhs.items():
            rows = []
            for i in range(start, start + step):
                a, b = own[e][0, i, k], theirs[e][0, i, k]
                rows += [jnp.where(first, a, b), jnp.where(first, b, a)]
            term = lax.dot_general(
                left,
                jnp.concatenate(rows, axis=0),
                (((1,), (1,)), ((), ())),
                preferred_element_type=F32,
            )
            total = term if total is None else total + term
        for i in range(start, start + step):
            row_mask = masks[pl.ds(n_ct * n_k + i, 1), pl.ds(0, 2 * vt)]
            kept = total[:, (i - start) * 2 * vt : (i - start + 1) * 2 * vt] * row_mask
            for d, out in enumerate(outs):
                out[i] = kept[d * vt : (d + 1) * vt].astype(out.dtype)


def join_kernel(*refs):
    refs[-1][...] = jnp.zeros_like(refs[-1])


def place_kernel(shifts, *refs):
    parts, (out, stage, sems) = refs, refs[-3:]
    tr, ct = lax.axis_index("tr"), lax.axis_index("ct")
    wide = parts[0].shape[2]
    half = lax.broadcasted_iota(jnp.int32, (1, wide), 1) < wide // 2
    straight = pair_bit(ct) == 1
    own_first = (tr & (3 - pair_bit(ct))) == 0
    places = []
    for by_core in shifts:
        shift = sum(jnp.where(ct == c, z, 0) for c, z in enumerate(by_core))
        places.append(pl.multiple_of(((tr // 4) ^ shift) * 2 * wide, 2 * wide))

    @pl.when(straight)
    def _():
        copies = []
        for n, at in enumerate(places):
            for m in range(2):
                lane = pl.multiple_of(at + jnp.where(own_first, m, 1 - m) * wide, wide)
                copies.append(
                    pltpu.make_async_copy(parts[2 * n + m], out.at[:, :, pl.ds(lane, wide)], sems.at[2 * n + m])
                )
                copies[-1].start()
        for copy in copies:
            copy.wait()

    @pl.when(jnp.logical_not(straight))
    def _():
        copies = []
        for n, at in enumerate(places):
            for i in range(out.shape[0]):
                a, b = parts[2 * n][i], parts[2 * n + 1][i]
                lo, hi = jnp.where(own_first, a, b), jnp.where(own_first, b, a)
                across = pltpu.roll(jnp.where(half, hi, lo).astype(F32), wide // 2, 1).astype(lo.dtype)
                stage[n, i, :, pl.ds(0, wide)] = jnp.where(half, lo, hi)
                stage[n, i, :, pl.ds(wide, wide)] = across
            copies.append(pltpu.make_async_copy(stage.at[n], out.at[:, :, pl.ds(at, 2 * wide)], sems.at[2 * n]))
            copies[-1].start()
        for copy in copies:
            copy.wait()


def per_device(n_tr, n_ct, amplitudes, cycle_integrals, pair_live):
    n_i, vt, n_k, cols = amplitudes.shape
    n_j = cycle_integrals.shape[2]
    n_local = n_i // n_ct
    n_z = n_tr // 4
    ct = lax.axis_index("ct")
    far = sorted(range(1, n_z), key=lambda z: -z)
    shared, split = far[: len(far) // n_ct * n_ct], far[len(far) // n_ct * n_ct :]
    groups = [shared[n : n + n_ct] for n in range(0, len(shared), n_ct)]
    shifts = [[group[c ^ e] for c in range(n_ct)] for group in groups for e in range(n_ct)]
    shifts += [[z] * n_ct for z in split] + [[0] * n_ct]

    def beside(c):
        return 3 - pair_bit(c)

    def over_ct(value, e):
        return lax.ppermute(value, "ct", [(c, c ^ e) for c in range(n_ct)])

    def over_tr(value, move, e=0):
        pairs = [(r * n_ct + c, (r ^ move(c ^ e)) * n_ct + (c ^ e)) for r in range(n_tr) for c in range(n_ct)]
        return lax.ppermute(value, ("tr", "ct"), pairs)

    def call(kernel, shape, inputs, after=(), gflop=0, dtype=jnp.bfloat16, count=None):
        result = jax.ShapeDtypeStruct(shape, dtype)
        return pl.pallas_call(
            kernel,
            out_shape=result if count is None else [result] * count,
            in_specs=[VMEM] * len(inputs) + [ANY] * len(after),
            out_specs=VMEM if count is None else [VMEM] * count,
            compiler_params=PARAMS,
            cost_estimate=cost(gflop),
        )(*inputs, *after)

    def pack(parts, after=(), gflop=0):
        shape = (sum(part.shape[0] for part in parts), *parts[0].shape[1:])
        return call(functools.partial(pack_kernel, len(parts)), shape, parts, after, gflop)

    own_w = jnp.transpose(cycle_integrals, (2, 0, 3, 1))
    masks = pl.pallas_call(
        functools.partial(masks_kernel, n_ct, n_k, n_local, vt),
        out_shape=jax.ShapeDtypeStruct((n_ct * n_k + n_local + 1, cols), F32),
        in_specs=[SMEM],
        out_specs=VMEM,
        compiler_params=PARAMS,
        cost_estimate=cost(),
    )(pair_live)

    by_group = jnp.transpose(amplitudes, (0, 2, 1, 3)).reshape(n_ct, n_local, n_k, vt, cols)
    given = [lax.dynamic_index_in_dim(by_group, ct ^ e, 0) for e in range(n_ct)]
    own_a = [given[0]] + [over_ct(given[e], e) for e in range(1, n_ct)]

    own_parts = pack([own_w] + [over_ct(own_w, e) for e in range(1, n_ct)])
    some = [over_tr(own_w, lambda c, z=z: 4 * z) for z in split]
    whole = [over_tr(own_parts, lambda c, group=group: 4 * group[c]) for group in groups]
    their_a = [over_tr(value, pair_bit, e) for e, value in enumerate(given)]
    whole = pack(whole, [masks], 3)
    some = some[0] if len(some) == 1 else pack(some)
    whole_side = [over_tr(whole, beside, e) for e in range(n_ct)]
    whole_rest = [over_ct(whole, e) for e in range(1, n_ct)]
    some_rest = [over_ct(some, e) for e in range(1, n_ct)]
    some_side = over_tr(pack([own_parts, some, *some_rest], their_a[1:]), beside)

    n_some = some.shape[0]
    of_group = [[(n, g * n_ct + (e ^ n)) for e in range(n_ct)] for g in range(len(groups)) for n in range(n_ct)]
    column = of_group + [[(n_ct + e, n) for e in range(n_ct)] for n in range(len(split))]
    column += [[(2 * n_ct, e) for e in range(n_ct)]]
    side_near = [[(0, n_ct + e * n_some + n) for e in range(n_ct)] for n in range(len(split))]
    side_near += [[(0, e) for e in range(n_ct)]]

    def blocks(tiles, arrays, after, gflop):
        kernel = functools.partial(blocks_kernel, n_ct, tiles)
        inputs = [masks, *own_a, *their_a, *arrays]
        return call(kernel, (n_local, vt, 2 * vt), inputs, after, gflop, count=len(tiles))

    near = blocks(column, [whole, *whole_rest, some, *some_rest, own_parts], [], 0)
    made = near[:1]
    near = [over_tr(b, lambda c, by=by: 4 * by[c]) if any(by) else b for b, by in zip(near, shifts)]
    side = blocks(of_group, whole_side, made, 9)
    made = side[:1]
    side = [over_tr(b, lambda c, by=by: 4 * by[c] + beside(c)) for b, by in zip(side, shifts)]
    late = blocks(side_near, [some_side], [*made, *near[:2]], 8)
    done = call(join_kernel, (8, 128), [], side, 10, F32)
    side += [over_tr(b, lambda c, by=by: 4 * by[c] + beside(c)) for b, by in zip(late, shifts[len(shared) :])]

    moved = [block for both in zip(near, side) for block in both]
    result = pl.pallas_call(
        functools.partial(place_kernel, shifts),
        out_shape=jax.ShapeDtypeStruct((n_local, vt, n_tr * vt), jnp.bfloat16),
        in_specs=[VMEM] * len(moved) + [ANY],
        out_specs=ANY,
        scratch_shapes=[
            pltpu.VMEM((n_z, n_local, vt, 4 * vt), jnp.bfloat16),
            pltpu.SemaphoreType.DMA((2 * n_z,)),
        ],
        compiler_params=PARAMS,
        cost_estimate=cost(),
    )(*moved, done)
    return result.reshape(n_local, vt, n_j, n_tr * vt)


def solution(mesh):
    return jax.shard_map(
        functools.partial(per_device, mesh.shape["tr"], mesh.shape["ct"]),
        mesh=mesh,
        in_specs=(P(None, "tr", None, "ct"), P(None, "ct", None, "tr"), P()),
        out_specs=P("ct", "tr", None, None),
        check_vma=False,
    )
```
